32 devices in a mesh: grp: 2 (over x), kern: 2 (over core), row: 8 (over z, y).
Axes of the slice: x: 2, y: 2, z: 4, core: 2. Of those that a mesh axis runs over, the one named last changes fastest.
Arguments:
- mask_levels: float32 [4096, 2048], P(('grp', 'row'), 'kern'), parts along dimension 0, may hold values from -6 to 6
- target_image: float32 [4096, 2048], P(('grp', 'row'), 'kern'), parts along dimension 0, may hold values from 0 to 1
- diffusion_index: int32 [128, 64], P(('grp', 'row'), 'kern'), parts along dimension 0, may hold values from 0 to 7
- diffusion_table: float32 [8], replicated, may hold values from 0.04 to 0.24
- kernel_weights: float32 [16], P('kern'), may hold values from 0.02 to 0.2
- kernel_spectra: float32 [2, 16, 256, 256], P(None, 'kern'), may hold values from -5 to 5
Outputs:
- gradient: float32 [4096, 2048], P(('grp', 'row'), 'kern'), parts along dimension 0
- resist: float32 [4096, 2048], P(('grp', 'row'), 'kern'), parts along dimension 0
The draws below stay inside these ranges and needn't reach their ends.
There are 2 independent parts, one for each index of `grp`. The reference program is written for one: setup_inputs(seed, part) draws one part's arguments, and reference() takes and returns one part's arrays. A program takes and returns all parts, laid end to end along the dimension named above; an argument that names none is the same for every part. Nothing has to cross between parts.
All inputs are finite; a program needn't handle non-finite values.
Results may differ from the reference program's by a relative error of at most 0.0003.
Values sent between devices are 32-bit elements; how exact they have to be, the bound alone decides.
A program may use at most 128 MiB of HBM per device.

```python
import math
import jax
import jax.numpy as jnp
from jax import lax

PIXELS = 2048
BAND = 256
KERNELS = 16
BLOCK = 32
LEVELS = 8
STEPS = 4


def touch_ends(values, key, least, largest):
    extent = values.shape
    spot = [jax.random.randint(jax.random.fold_in(key, axis), (), 0, extent[axis]) for axis in range(len(extent))]
    values = values.at[tuple(spot)].set(least)
    longest = extent.index(max(extent))
    spot[longest] = (spot[longest] + 1) % extent[longest]
    return values.at[tuple(spot)].set(largest)


def block_scale(stream_key, shape, cuts, least, largest):
    loudness = 1.0
    for axis_at, parts in cuts:
        steps = jax.random.uniform(jax.random.fold_in(jax.random.fold_in(stream_key, 6), axis_at), (parts,), jnp.float32, least / len(cuts), largest / len(cuts))
        loudness = loudness * jnp.repeat(jnp.exp(steps), shape[axis_at] // parts).reshape((-1,) + (1,) * (len(shape) - 1 - axis_at))
    return loudness


def scatter_about(key, dims, spread, limit, cuts=(), kind=jnp.bfloat16):
    gain = block_scale(key, dims, cuts, -0.22, 0.18) if cuts else 1.0
    drawn = jax.random.normal(key, dims, jnp.float32) * spread * gain
    return jnp.minimum(jnp.maximum(drawn, -limit), limit).astype(kind)


def setup_inputs(seed: int = 0, part: int = 0) -> dict:
    streams_of = jax.random.split(jax.random.key(seed), 7)
    part_keys = jax.random.split(jax.random.fold_in(streams_of[6], part), 7)
    mask_levels = scatter_about(part_keys[0], (PIXELS, PIXELS), 1.0, 6.0, ((0, 8), (1, 2)), jnp.float32)
    target_image = jnp.clip(1.0 * jax.random.uniform(part_keys[1], (PIXELS, PIXELS), jnp.float32) ** block_scale(part_keys[1], (PIXELS, PIXELS), ((0, 8), (1, 2)), -0.2, 0.2), 0.0, 1.0)
    diffusion_index = touch_ends(jax.random.randint(part_keys[2], (PIXELS // BLOCK, PIXELS // BLOCK), 0, LEVELS), jax.random.fold_in(part_keys[2], 1), 0, LEVELS - 1).astype(jnp.int32)
    diffusion_table = jnp.clip(jnp.exp(jax.random.uniform(streams_of[3], (LEVELS,), jnp.float32, math.log(0.04), math.log(0.24))), 0.04, 0.24)
    kernel_weights = jnp.clip(jnp.exp(math.log(0.2) - 2.3025851 * jax.random.uniform(streams_of[4], (KERNELS,), jnp.float32) ** block_scale(streams_of[4], (KERNELS,), ((0, 2),), -0.2, 0.2)), 0.02, 0.2)
    kernel_spectra = scatter_about(streams_of[5], (2, KERNELS, BAND, BAND), 0.7, 5.0, ((1, 2),), jnp.float32)
    return dict(mask_levels=mask_levels, target_image=target_image, diffusion_index=diffusion_index, diffusion_table=diffusion_table, kernel_weights=kernel_weights, kernel_spectra=kernel_spectra)


steepness = 8.0
threshold = 0.5

def diffuse(values, root_field):
    padded = jnp.pad(values, 1)
    padded_root = jnp.pad(root_field, 1)
    height, breadth = values.shape
    running = jnp.zeros_like(values)
    for offset_row, offset_col in ((0, 1), (2, 1), (1, 0), (1, 2)):
        beside = padded[offset_row:offset_row + height, offset_col:offset_col + breadth]
        beside_root = padded_root[offset_row:offset_row + height, offset_col:offset_col + breadth]
        running = running + beside_root * (beside - values)
    return values + root_field * running

def resist_image(mask_levels, diffusion_index, diffusion_table, kernel_weights, kernel_spectra):
    transmit = jnp.tanh(mask_levels)
    band_start = PIXELS // 2 - BAND // 2
    spectrum = jnp.fft.fftshift(jnp.fft.fft2(transmit))[band_start:band_start + BAND, band_start:band_start + BAND] / PIXELS

    def add_kernel(running, pieces):
        real_part, imag_part, weight = pieces
        pupil_spec = real_part + 1j * imag_part
        padded = jnp.zeros((PIXELS, PIXELS), spectrum.dtype)
        padded = padded.at[band_start:band_start + BAND, band_start:band_start + BAND].set(pupil_spec * spectrum)
        kernel_field = jnp.fft.ifft2(jnp.fft.ifftshift(padded)) * (PIXELS * PIXELS / BAND)
        return (running + weight * (kernel_field.real ** 2 + kernel_field.imag ** 2), None)
    intensity, ignored = lax.scan(jax.checkpoint(add_kernel), jnp.zeros((PIXELS, PIXELS), jnp.float32), (kernel_spectra[0], kernel_spectra[1], kernel_weights))
    block_root = jnp.sqrt(diffusion_table)[diffusion_index]
    root_field = jnp.repeat(jnp.repeat(block_root, BLOCK, axis=0), BLOCK, axis=1)
    acid_level = intensity
    for iteration in range(STEPS):
        acid_level = diffuse(acid_level, root_field)
    return jax.nn.sigmoid(steepness * (acid_level - threshold))

def reference(mask_levels, target_image, diffusion_index, diffusion_table, kernel_weights, kernel_spectra):

    def loss_of(levels):
        resist = resist_image(levels, diffusion_index, diffusion_table, kernel_weights, kernel_spectra)
        return (jnp.sum((resist - target_image) ** 2), resist)
    loss_value, pull_back, resist = jax.vjp(loss_of, mask_levels, has_aux=True)
    gradient, = pull_back(jnp.ones_like(loss_value))
    return (gradient, resist)
```

```python
import numpy as np
import jax
import jax.numpy as jnp
from jax import lax
from jax.sharding import PartitionSpec as P

PIXELS = 2048
BAND = 256
BLOCK = 32
STEPS = 4
HALF = BAND // 2
GRID = 2 * BAND
HALO = 2 * STEPS
LANES = 128
steepness = 8.0
threshold = 0.5
high = lax.Precision.HIGHEST


def mm(a, b):
    return jnp.dot(a, b, precision=high, preferred_element_type=jnp.float32)


def mm_ta(a, b):
    return lax.dot_general(a, b, (((0,), (0,)), ((), ())), precision=high, preferred_element_type=jnp.float32)


def mm_tb(a, b):
    return lax.dot_general(a, b, (((1,), (1,)), ((), ())), precision=high, preferred_element_type=jnp.float32)


def mask_table():
    n = np.arange(HALF)
    f = np.concatenate([n, -(n + 1)])
    angle = 2 * np.pi / PIXELS * ((f[:, None] * np.arange(PIXELS)[None, :]) % PIXELS)
    return np.cos(angle), np.sin(angle)


def half_table(positions):
    n = np.arange(HALF)
    angle = np.pi / PIXELS * (((2 * n + 1)[:, None] * positions[None, :]) % (2 * PIXELS))
    return np.concatenate([np.cos(angle), np.sin(angle)], 0)


def interpolation_table():
    d = np.arange(PIXELS)[:, None] - (PIXELS // GRID) * np.arange(GRID)[None, :]
    d = d % PIXELS
    safe = np.where(d == 0, 1, d)
    u = np.sin(2 * np.pi * ((BAND * safe) % PIXELS) / PIXELS) / (GRID * np.tan(np.pi * safe / PIXELS))
    return np.where(d == 0, 1.0, u)


def const(x):
    return jnp.asarray(x.astype(np.float32))


def fold(h):
    h = jnp.concatenate([h[..., HALF:, :], jnp.flip(h[..., :HALF, :], -2)], -2)
    return jnp.concatenate([h[..., HALF:], jnp.flip(h[..., :HALF], -1)], -1)


def diffuse(acid, root):
    up = jnp.roll(root, 1, 0) * (jnp.roll(acid, 1, 0) - acid)
    up = up + jnp.roll(root, -1, 0) * (jnp.roll(acid, -1, 0) - acid)
    up = up + jnp.roll(root, 1, 1) * (jnp.roll(acid, 1, 1) - acid)
    up = up + jnp.roll(root, -1, 1) * (jnp.roll(acid, -1, 1) - acid)
    return acid + root * up


def quads(g):
    a, b, c, d = g[..., :HALF, :HALF], g[..., :HALF, HALF:], g[..., HALF:, :HALF], g[..., HALF:, HALF:]
    return a + b + c + d, a + c - b - d, a + b - c - d, a - b - c + d


def join(a, b, c, d):
    return jnp.concatenate([jnp.concatenate([a, b], -1), jnp.concatenate([c, d], -1)], -2)


def body(mask_levels, target_image, diffusion_index, diffusion_table, kernel_weights, kernel_spectra):
    height, breadth = mask_levels.shape
    rows_n, cols_n = lax.axis_size("row"), lax.axis_size("kern")
    row, col = lax.axis_index("row"), lax.axis_index("kern")
    row_start, col_start = row * height, col * breadth
    tall, wide = height + 2 * HALO, breadth + LANES

    ct, st = mask_table()
    cut_rows = lambda t, s, n: lax.dynamic_slice_in_dim(t, s, n, 0)
    col_tab = cut_rows(const(np.concatenate([ct.T, st.T], 1)), col_start, breadth)
    row_tab = cut_rows(const(np.concatenate([ct.T, st.T], 1)), row_start, height)

    row_pos = np.concatenate([np.arange(rows_n * height), [0] * 0])
    base = half_table(np.arange(-HALO, PIXELS + HALO)).T
    r_mid = cut_rows(const(base), row_start, tall)
    r_tab = jnp.concatenate([r_mid[HALO:], r_mid[:HALO]], 0)
    t_tab = const(half_table(np.arange(GRID) * (PIXELS // GRID)))
    inter = interpolation_table()
    inter = np.concatenate([inter[-LANES // 2:], inter, inter[:LANES // 2]], 0)
    u_mid = cut_rows(const(inter), col_start, wide)
    u_tab = jnp.concatenate([u_mid[LANES // 2:], u_mid[:LANES // 2]], 0)

    transmit = jnp.tanh(mask_levels)
    halfway = mm(transmit, col_tab)
    prod = mm_ta(row_tab, halfway)
    scale = 1.0 / (PIXELS * BAND)
    s_re = (prod[:BAND, :BAND] - prod[BAND:, BAND:]) * scale
    s_im = -(prod[BAND:, :BAND] + prod[:BAND, BAND:]) * scale
    s_re, s_im = lax.psum((s_re, s_im), ("kern", "row"))

    hot = (diffusion_index[:, :, None] == jnp.arange(diffusion_table.shape[0], dtype=jnp.int32)).astype(jnp.float32)
    block_root = jnp.sum(hot * jnp.sqrt(diffusion_table), -1)
    br, bc = block_root.shape
    root = jnp.broadcast_to(block_root[:, None, :, None], (br, BLOCK, bc, BLOCK)).reshape(height, breadth)
    both = jnp.stack([target_image, root])
    up = [(i, (i + 1) % cols_n) for i in range(cols_n - 1)]
    dn = [(j, i) for i, j in up]
    right = lax.ppermute(both[:, :, : LANES // 2], "kern", dn)
    left = lax.ppermute(both[:, :, breadth - LANES // 2:], "kern", up)
    both = jnp.concatenate([both, right, left], 2)
    up = [(i, i + 1) for i in range(rows_n - 1)]
    dn = [(j, i) for i, j in up]
    below = lax.ppermute(both[:, :HALO], "row", dn)
    above = lax.ppermute(both[:, height - HALO:], "row", up)
    both = jnp.concatenate([both, below, above], 1)
    target, root = both[0], both[1]

    h = fold(kernel_spectra)
    h_re, h_im = h[0], h[1]
    g_re = h_re * s_re - h_im * s_im
    g_im = h_re * s_im + h_im * s_re
    ee_r, eo_r, oe_r, oo_r = quads(g_re)
    ee_i, eo_i, oe_i, oo_i = quads(g_im)
    m = jnp.stack([join(ee_r, -eo_i, -oe_i, -oo_r), join(ee_i, eo_r, oe_r, -oo_i)])
    left_part = jnp.einsum("ip,ckpq->ckiq", r_tab, m, precision=high, preferred_element_type=jnp.float32)
    fields = jnp.einsum("ckiq,qj->ckij", left_part, t_tab, precision=high, preferred_element_type=jnp.float32)
    power = jnp.sum(kernel_weights[:, None, None] * (fields[0] ** 2 + fields[1] ** 2), 0)
    power = lax.psum(power, "kern")
    acid = mm_tb(power, u_tab)
    for _ in range(STEPS):
        acid = diffuse(acid, root)
    resist = jax.nn.sigmoid(steepness * (acid - threshold))
    sens = 2.0 * steepness * resist * (1.0 - resist) * (resist - target)
    for _ in range(STEPS):
        sens = diffuse(sens, root)
    q_grid = mm(sens[:height, :breadth], u_tab[:breadth])
    q_grid = lax.psum(q_grid, "kern")
    d_field = (2.0 * kernel_weights)[:, None, None] * q_grid * fields[:, :, :height]
    d_left = jnp.einsum("ckij,qj->ckiq", d_field, t_tab, precision=high, preferred_element_type=jnp.float32)
    d_m = jnp.einsum("ip,ckiq->ckpq", r_tab[:height], d_left, precision=high, preferred_element_type=jnp.float32)

    dr, di = d_m[0], d_m[1]
    part = lambda x: (x[..., :HALF, :HALF], x[..., :HALF, HALF:], x[..., HALF:, :HALF], x[..., HALF:, HALF:])
    ra, rb, rc, rd = part(dr)
    ia, ib, ic, id_ = part(di)

    def spread(ee, eo, oe, oo):
        return join(ee + eo + oe + oo, ee - eo + oe - oo, ee + eo - oe - oo, ee - eo - oe + oo)

    dg_re = spread(ra, ib, ic, -rd)
    dg_im = spread(ia, -rb, -rc, -id_)
    ds_re = jnp.sum(h_re * dg_re + h_im * dg_im, 0)
    ds_im = jnp.sum(h_re * dg_im - h_im * dg_re, 0)
    ds_re, ds_im = lax.psum((ds_re, ds_im), ("kern", "row"))
    block = jnp.concatenate([jnp.concatenate([ds_re, -ds_im], 1), jnp.concatenate([-ds_im, -ds_re], 1)], 0) * scale
    grad = mm_tb(mm(row_tab, block), col_tab)
    gradient = grad * (1.0 - transmit * transmit)
    return gradient, resist[:height, :breadth]


def solution(mesh):
    return jax.shard_map(
        body,
        mesh=mesh,
        in_specs=(
            P(("grp", "row"), "kern"),
            P(("grp", "row"), "kern"),
            P(("grp", "row"), "kern"),
            P(),
            P("kern"),
            P(None, "kern", None, None),
        ),
        out_specs=(P(("grp", "row"), "kern"), P(("grp", "row"), "kern")),
        check_vma=False,
    )
```

```python
import numpy as np
import jax
import jax.numpy as jnp
from jax import lax
from jax.experimental import pallas as pl
from jax.experimental.pallas import tpu as pltpu
from jax.sharding import PartitionSpec as P

PIXELS = 2048
BAND = 256
BLOCK = 32
STEPS = 4
HALF = BAND // 2
GRID = 2 * BAND
HALO = 2 * STEPS
LANES = 128
steepness = 8.0
threshold = 0.5
MESH = pl.DeviceIdType.MESH
NN = ((1,), (0,))
NT = ((1,), (1,))
TN = ((0,), (0,))


def mask_table():
    n = np.arange(HALF)
    f = np.concatenate([n, -(n + 1)])
    angle = 2 * np.pi / PIXELS * ((f[:, None] * np.arange(PIXELS)[None, :]) % PIXELS)
    return np.cos(angle), np.sin(angle)


def half_table(positions):
    n = np.arange(HALF)
    angle = np.pi / PIXELS * (((2 * n + 1)[:, None] * positions[None, :]) % (2 * PIXELS))
    return np.concatenate([np.cos(angle), np.sin(angle)], 0)


def interpolation_table():
    d = np.arange(PIXELS)[:, None] - (PIXELS // GRID) * np.arange(GRID)[None, :]
    d = d % PIXELS
    safe = np.where(d == 0, 1, d)
    u = np.sin(2 * np.pi * ((BAND * safe) % PIXELS) / PIXELS) / (GRID * np.tan(np.pi * safe / PIXELS))
    return np.where(d == 0, 1.0, u)


def halves(x):
    x = x.astype(np.float32)
    hi = x.astype(jnp.bfloat16)
    lo = (x - hi.astype(np.float32)).astype(jnp.bfloat16)
    return jnp.asarray(hi), jnp.asarray(lo)


def fold_matrix():
    a = np.arange(BAND)
    p = np.zeros((BAND, BAND))
    p[a, np.where(a < HALF, a + HALF, BAND - 1 - a)] = 1.0
    return jnp.asarray(p.astype(jnp.bfloat16)), jnp.asarray(p.T.astype(jnp.bfloat16))


def quads(g):
    a, b, c, d = g[..., :HALF, :HALF], g[..., :HALF, HALF:], g[..., HALF:, :HALF], g[..., HALF:, HALF:]
    return a + b + c + d, a + c - b - d, a + b - c - d, a - b - c + d


def join(a, b, c, d):
    return jnp.concatenate([jnp.concatenate([a, b], -1), jnp.concatenate([c, d], -1)], -2)


def spread(ee, eo, oe, oo):
    return join(ee + eo + oe + oo, ee - eo + oe - oo, ee + eo - oe - oo, ee - eo - oe + oo)


def split(x):
    hi = x.astype(jnp.bfloat16)
    return hi, (x - hi.astype(jnp.float32)).astype(jnp.bfloat16)


def dot(a, b, dims):
    return lax.dot_general(a, b, (dims, ((), ())), preferred_element_type=jnp.float32)


def dot3(a, b, dims=NN):
    return dot(a[0], b[0], dims) + dot(a[0], b[1], dims) + dot(a[1], b[0], dims)


def diffuse(acid, vertical, across):
    fv = vertical * (pltpu.roll(acid, 1, 0) - acid)
    fh = across * (pltpu.roll(acid, 1, 1) - acid)
    tall, wide = acid.shape
    return acid + (fv - pltpu.roll(fv, tall - 1, 0)) + (fh - pltpu.roll(fh, wide - 1, 1))


def kernel(rows_n, mask, target, root_rows, weights, spectra, m_hi, m_lo, u_hi, u_lo, t_hi, t_lo, r_all, p_fwd, p_bwd,
           gradient, resist_out,
           spec, full1, full2, pair_in, part, rs_in, both, h_in, h, fields, power, power_in, grid, grid_in,
           row_hi, row_lo, col_hi, col_lo, ut_hi, ut_lo, r_buf, transmit,
           local_sem, pair_send, pair_recv, rs_send, rs_recv, ag_send, ag_recv):
    height, breadth = mask.shape
    tall, wide = both.shape[1:]
    kernels = h.shape[1]
    row, col = lax.axis_index("row"), lax.axis_index("kern")
    partner = 1 - col
    row_start, col_start = row * height, pl.multiple_of(col * breadth, LANES)
    slab = pl.multiple_of(breadth - LANES * col, LANES)

    local = [
        pltpu.make_async_copy(m_hi.at[pl.ds(col_start, breadth)], col_hi, local_sem.at[0]),
        pltpu.make_async_copy(m_lo.at[pl.ds(col_start, breadth)], col_lo, local_sem.at[1]),
        pltpu.make_async_copy(m_hi.at[pl.ds(row_start, height)], row_hi, local_sem.at[2]),
        pltpu.make_async_copy(m_lo.at[pl.ds(row_start, height)], row_lo, local_sem.at[3]),
        pltpu.make_async_copy(spectra, h_in, local_sem.at[4]),
        pltpu.make_async_copy(r_all.at[pl.ds(row_start + HALO, tall - HALO)], r_buf.at[pl.ds(0, tall - HALO)], local_sem.at[5]),
        pltpu.make_async_copy(r_all.at[pl.ds(row_start, HALO)], r_buf.at[pl.ds(tall - HALO, HALO)], local_sem.at[6]),
        pltpu.make_async_copy(u_hi.at[:, pl.ds(col_start, breadth)], ut_hi.at[:, pl.ds(0, breadth)], local_sem.at[7]),
        pltpu.make_async_copy(u_lo.at[:, pl.ds(col_start, breadth)], ut_lo.at[:, pl.ds(0, breadth)], local_sem.at[8]),
        pltpu.make_async_copy(u_hi.at[:, pl.ds(slab, LANES)], ut_hi.at[:, pl.ds(breadth, LANES)], local_sem.at[9]),
        pltpu.make_async_copy(u_lo.at[:, pl.ds(slab, LANES)], ut_lo.at[:, pl.ds(breadth, LANES)], local_sem.at[10]),
    ]
    for copy in local:
        copy.start()

    barrier = pltpu.get_barrier_semaphore()
    pl.semaphore_signal(barrier, inc=1, device_id={"kern": partner}, device_id_type=MESH)
    for o in range(1, rows_n):
        pl.semaphore_signal(barrier, inc=1, device_id={"row": lax.rem(row + o, rows_n)}, device_id_type=MESH)

    both[0, pl.ds(0, height), pl.ds(0, breadth)] = target[...]
    for b in range(root_rows.shape[0]):
        both[1, pl.ds(b * BLOCK, BLOCK), pl.ds(0, breadth)] = jnp.broadcast_to(root_rows[b : b + 1, :], (BLOCK, breadth))
    pl.semaphore_wait(barrier, rows_n)

    def to_pair(src, dst, n):
        return pltpu.make_async_remote_copy(
            src_ref=src, dst_ref=dst, send_sem=pair_send.at[n], recv_sem=pair_recv.at[n],
            device_id={"kern": partner}, device_id_type=MESH)

    edge = pl.multiple_of((breadth - LANES) * partner, LANES)
    side = to_pair(both.at[:, pl.ds(0, height), pl.ds(edge, LANES)], both.at[:, pl.ds(0, height), pl.ds(breadth, LANES)], 0)
    side.start()

    def to_row(src, dst, peer, send, recv, n):
        return pltpu.make_async_remote_copy(
            src_ref=src, dst_ref=dst, send_sem=send.at[n], recv_sem=recv.at[n],
            device_id={"row": peer}, device_id_type=MESH)

    chunk = BAND // rows_n

    def allreduce(at, src, full, beside_pair=None, beside_scatter=None, beside_gather=None):
        swap = to_pair(src.at[pl.ds(partner * BAND, BAND)], pair_in.at[at], 1 + 2 * at)
        swap.start()
        if beside_pair is not None:
            beside_pair()
        swap.wait()
        part[at] = src[pl.ds(col * BAND, BAND)] + pair_in[at]
        copies = []
        for o in range(1, rows_n):
            peer = lax.rem(row + o, rows_n)
            copies.append(to_row(part.at[at, pl.ds(peer * chunk, chunk)], rs_in.at[at, o - 1], peer, rs_send.at[at], rs_recv.at[at], o - 1))
            copies[-1].start()
        if beside_scatter is not None:
            beside_scatter()
        for copy in copies:
            copy.wait()
        total = part[at, pl.ds(row * chunk, chunk)]
        for o in range(1, rows_n):
            total = total + rs_in[at, o - 1]
        mine = pl.ds(col * BAND + row * chunk, chunk)
        full[mine] = total
        copies = []
        for o in range(1, rows_n):
            peer = lax.rem(row + o, rows_n)
            copies.append(to_row(full.at[mine], full.at[mine], peer, ag_send.at[at], ag_recv.at[at], o - 1))
            copies[-1].start()
        if beside_gather is not None:
            beside_gather()
        for copy in copies:
            copy.wait()
        half = pl.ds(col * BAND, BAND)
        swap = to_pair(full.at[half], full.at[half], 2 + 2 * at)
        swap.start()
        swap.wait()

    scale = 1.0 / (PIXELS * BAND)
    transmit[...] = jnp.tanh(mask[...])
    for copy in local[:4]:
        copy.wait()
    col_tab = (col_hi[...], col_lo[...])
    row_tab = (row_hi[...], row_lo[...])
    halfway = dot3(split(transmit[...]), col_tab)
    prod = dot3(row_tab, split(halfway), TN)
    spec[pl.ds(0, BAND)] = (prod[:BAND, :BAND] - prod[BAND:, BAND:]) * scale
    spec[pl.ds(BAND, BAND)] = -(prod[BAND:, :BAND] + prod[:BAND, BAND:]) * scale

    def fold(first, count):
        def step(k, _):
            for c in range(2):
                hi, lo = split(h_in[c, k])
                mid = split(dot(p_fwd[...], hi, NN) + dot(p_fwd[...], lo, NN))
                h[c, k] = dot(mid[0], p_bwd[...], NN) + dot(mid[1], p_bwd[...], NN)
            return 0
        lax.fori_loop(first, first + count, step, 0)

    ends = []

    def beside_pair():
        side.wait()
        ends.append(to_row(both.at[:, pl.ds(0, HALO)], both.at[:, pl.ds(height, HALO)], lax.rem(row + rows_n - 1, rows_n), rs_send.at[2], rs_recv.at[2], 0))
        ends.append(to_row(both.at[:, pl.ds(height - HALO, HALO)], both.at[:, pl.ds(height + HALO, HALO)], lax.rem(row + 1, rows_n), rs_send.at[2], rs_recv.at[2], 1))
        for copy in ends:
            copy.start()
        for copy in local[4:]:
            copy.wait()

    allreduce(0, spec, full1, beside_pair, lambda: fold(0, kernels // 2), lambda: fold(kernels // 2, kernels - kernels // 2))

    t_tab = (t_hi[...], t_lo[...])
    r_tab = split(r_buf[...])
    power[...] = jnp.zeros_like(power)

    def forward(k, _):
        h_re, h_im = h[0, k], h[1, k]
        s_re, s_im = full1[pl.ds(0, BAND)], full1[pl.ds(BAND, BAND)]
        ee_r, eo_r, oe_r, oo_r = quads(h_re * s_re - h_im * s_im)
        ee_i, eo_i, oe_i, oo_i = quads(h_re * s_im + h_im * s_re)
        square = 0.0
        for c, m in enumerate((join(ee_r, -eo_i, -oe_i, -oo_r), join(ee_i, eo_r, oe_r, -oo_i))):
            field = dot3(split(dot3(r_tab, split(m))), t_tab)
            fields[k, c] = field
            square = square + field * field
        power[...] += weights[k] * square
        return 0

    lax.fori_loop(0, kernels, forward, 0)
    swap = to_pair(power, power_in, 5)
    swap.start()

    for copy in ends:
        copy.wait()
    at_row = lax.broadcasted_iota(jnp.int32, (tall, wide), 0)
    at_col = lax.broadcasted_iota(jnp.int32, (tall, wide), 1)
    first, last = row == 0, row == rows_n - 1
    outside = (at_row >= height + HALO) & first
    outside = outside | ((at_row >= height) & (at_row < height + HALO) & last)
    outside = outside | ((at_col >= breadth + LANES // 2) & (col == 0))
    outside = outside | ((at_col >= breadth) & (at_col < breadth + LANES // 2) & (col == 1))
    root = jnp.where(outside, 0.0, both[1])
    vertical = root * pltpu.roll(root, 1, 0)
    across = root * pltpu.roll(root, 1, 1)
    swap.wait()

    u_tab = (ut_hi[...], ut_lo[...])
    acid = dot3(split(power[...] + power_in[...]), u_tab)
    for _ in range(STEPS):
        acid = diffuse(acid, vertical, across)
    resist = 1.0 / (1.0 + jnp.exp(-steepness * (acid - threshold)))
    resist_out[...] = resist[:height, :breadth]
    sens = 2.0 * steepness * resist * (1.0 - resist) * (resist - both[0])
    for _ in range(STEPS):
        sens = diffuse(sens, vertical, across)
    grid[...] = dot3(split(sens[:height, :breadth]), (u_tab[0][:, :breadth], u_tab[1][:, :breadth]), NT)
    swap = to_pair(grid, grid_in, 6)
    swap.start()
    r_back = split(r_buf[pl.ds(0, height)].T)
    spec[...] = jnp.zeros_like(spec)
    swap.wait()
    grid[...] = 2.0 * (grid[...] + grid_in[...])

    def backward(k, _):
        parts = []
        for c in range(2):
            d = (weights[k] * grid[...]) * fields[k, c, pl.ds(0, height)]
            d = dot3(r_back, split(dot3(split(d), t_tab, NT)))
            parts.append((d[:HALF, :HALF], d[:HALF, HALF:], d[HALF:, :HALF], d[HALF:, HALF:]))
        (ra, rb, rc, rd), (ia, ib, ic, id_) = parts
        dg_re = spread(ra, ib, ic, -rd)
        dg_im = spread(ia, -rb, -rc, -id_)
        h_re, h_im = h[0, k], h[1, k]
        spec[pl.ds(0, BAND)] += h_re * dg_re + h_im * dg_im
        spec[pl.ds(BAND, BAND)] += h_re * dg_im - h_im * dg_re
        return 0

    lax.fori_loop(0, kernels, backward, 0)
    allreduce(1, spec, full2)
    ds_re, ds_im = full2[pl.ds(0, BAND)] * scale, full2[pl.ds(BAND, BAND)] * scale
    block = join(ds_re, -ds_im, -ds_im, -ds_re)
    grad = dot3(split(dot3(row_tab, split(block))), col_tab, NT)
    gradient[...] = grad * (1.0 - transmit[...] * transmit[...])


def body(mask_levels, target_image, diffusion_index, diffusion_table, kernel_weights, kernel_spectra):
    height, breadth = mask_levels.shape
    rows_n, cols_n = lax.axis_size("row"), lax.axis_size("kern")
    assert cols_n == 2
    tall, wide = height + 2 * HALO, breadth + LANES
    kernels = kernel_weights.shape[0]
    ct, st = mask_table()
    m_hi, m_lo = halves(np.concatenate([ct.T, st.T], 1))
    u_hi, u_lo = halves(interpolation_table().T)
    t_hi, t_lo = halves(half_table(np.arange(GRID) * (PIXELS // GRID)))
    r_all = jnp.asarray(half_table(np.arange(-HALO, PIXELS + HALO)).T.astype(np.float32))
    p_fwd, p_bwd = fold_matrix()
    hot = (diffusion_index[:, :, None] == jnp.arange(diffusion_table.shape[0], dtype=jnp.int32)).astype(jnp.float32)
    block_root = jnp.sum(hot * jnp.sqrt(diffusion_table), -1)
    root_rows = jnp.repeat(block_root, BLOCK, axis=1)
    f32, bf16 = jnp.float32, jnp.bfloat16
    vmem, hbm, smem = (pl.BlockSpec(memory_space=s) for s in (pltpu.VMEM, pl.ANY, pltpu.SMEM))
    V = pltpu.VMEM
    D = pltpu.SemaphoreType.DMA
    peers = max(rows_n - 1, 2)
    return pl.pallas_call(
        lambda *refs: kernel(rows_n, *refs),
        out_shape=(jax.ShapeDtypeStruct((height, breadth), f32),) * 2,
        in_specs=[vmem, vmem, vmem, smem, hbm, hbm, hbm, hbm, hbm, vmem, vmem, hbm, vmem, vmem],
        out_specs=(vmem, vmem),
        scratch_shapes=[
            V((2 * BAND, BAND), f32), V((2 * BAND, BAND), f32), V((2 * BAND, BAND), f32),
            V((2, BAND, BAND), f32), V((2, BAND, BAND), f32), V((2, peers, BAND // rows_n, BAND), f32),
            V((2, tall, wide), f32), V(kernel_spectra.shape, f32), V(kernel_spectra.shape, f32),
            V((kernels, 2, tall, GRID), f32), V((tall, GRID), f32), V((tall, GRID), f32),
            V((height, GRID), f32), V((height, GRID), f32),
            V((height, 2 * BAND), bf16), V((height, 2 * BAND), bf16),
            V((breadth, 2 * BAND), bf16), V((breadth, 2 * BAND), bf16),
            V((GRID, wide), bf16), V((GRID, wide), bf16), V((tall, BAND), f32), V((height, breadth), f32),
            D((11,)), D((7,)), D((7,)), D((3, peers)), D((3, peers)), D((2, peers)), D((2, peers)),
        ],
        compiler_params=pltpu.CompilerParams(collective_id=0, has_side_effects=True, vmem_limit_bytes=60 * 2**20),
        name="resist_gradient",
    )(mask_levels, target_image, root_rows, kernel_weights, kernel_spectra, m_hi, m_lo, u_hi, u_lo, t_hi, t_lo, r_all, p_fwd, p_bwd)


def solution(mesh):
    return jax.shard_map(
        body,
        mesh=mesh,
        in_specs=(
            P(("grp", "row"), "kern"),
            P(("grp", "row"), "kern"),
            P(("grp", "row"), "kern"),
            P(),
            P("kern"),
            P(None, "kern", None, None),
        ),
        out_specs=(P(("grp", "row"), "kern"), P(("grp", "row"), "kern")),
        check_vma=False,
    )
```

```python
import numpy as np
import jax
import jax.numpy as jnp
from jax import lax
from jax.experimental import pallas as pl
from jax.experimental.pallas import tpu as pltpu
from jax.sharding import PartitionSpec as P

PIXELS = 2048
BAND = 256
BLOCK = 32
STEPS = 4
HALF = BAND // 2
GRID = 2 * BAND
HALO = 2 * STEPS
LANES = 128
steepness = 8.0
threshold = 0.5
MESH = pl.DeviceIdType.MESH
NN = ((1,), (0,))
NT = ((1,), (1,))
TN = ((0,), (0,))


def mask_table():
    n = np.arange(HALF)
    f = np.concatenate([n, -(n + 1)])
    angle = 2 * np.pi / PIXELS * ((f[:, None] * np.arange(PIXELS)[None, :]) % PIXELS)
    return np.cos(angle), np.sin(angle)


def half_table(positions):
    n = np.arange(HALF)
    angle = np.pi / PIXELS * (((2 * n + 1)[:, None] * positions[None, :]) % (2 * PIXELS))
    return np.concatenate([np.cos(angle), np.sin(angle)], 0)


def interpolation_table():
    d = np.arange(PIXELS)[:, None] - (PIXELS // GRID) * np.arange(GRID)[None, :]
    d = d % PIXELS
    safe = np.where(d == 0, 1, d)
    u = np.sin(2 * np.pi * ((BAND * safe) % PIXELS) / PIXELS) / (GRID * np.tan(np.pi * safe / PIXELS))
    return np.where(d == 0, 1.0, u)


def halves(x):
    x = x.astype(np.float32)
    hi = x.astype(jnp.bfloat16)
    lo = (x - hi.astype(np.float32)).astype(jnp.bfloat16)
    return jnp.asarray(hi), jnp.asarray(lo)


def fold_matrix():
    a = np.arange(BAND)
    p = np.zeros((BAND, BAND))
    p[a, np.where(a < HALF, a + HALF, BAND - 1 - a)] = 1.0
    return jnp.asarray(p.astype(jnp.bfloat16)), jnp.asarray(p.T.astype(jnp.bfloat16))


def quads(g):
    a, b, c, d = g[..., :HALF, :HALF], g[..., :HALF, HALF:], g[..., HALF:, :HALF], g[..., HALF:, HALF:]
    return a + b + c + d, a + c - b - d, a + b - c - d, a - b - c + d


def join(a, b, c, d):
    return jnp.concatenate([jnp.concatenate([a, b], -1), jnp.concatenate([c, d], -1)], -2)


def spread(ee, eo, oe, oo):
    return join(ee + eo + oe + oo, ee - eo + oe - oo, ee + eo - oe - oo, ee - eo - oe + oo)


def split(x):
    hi = x.astype(jnp.bfloat16)
    return hi, (x - hi.astype(jnp.float32)).astype(jnp.bfloat16)


def dot(a, b, dims):
    return lax.dot_general(a, b, (dims, ((), ())), preferred_element_type=jnp.float32)


def dot3(a, b, dims=NN):
    return dot(a[0], b[0], dims) + dot(a[0], b[1], dims) + dot(a[1], b[0], dims)


def diffuse(ping, pong, coefs):
    tall, wide = ping.shape[0] - 2 * HALO, ping.shape[1]

    def step(src, dst):
        for at in range(HALO, HALO + tall, 16):
            x = src[at : at + 16, :]
            here = [c[at : at + 16, :] for c in coefs]
            moved = here[0] * (src[at - 1 : at + 15, :] - x) + here[1] * (src[at + 1 : at + 17, :] - x)
            moved = moved + here[2] * (pltpu.roll(x, 1, 1) - x) + here[3] * (pltpu.roll(x, wide - 1, 1) - x)
            dst[at : at + 16, :] = x + moved

    def twice(_, carry):
        step(ping, pong)
        step(pong, ping)
        return carry

    lax.fori_loop(0, STEPS // 2, twice, 0)


def linear(x, height):
    pad = jnp.zeros((HALO, x.shape[1]), x.dtype)
    return jnp.concatenate([pad, x[height + HALO :], x[: height + HALO], pad], 0)


def kernel(rows_n, mask, target, levels, level_values, weights, spectra, m_hi, m_lo, u_hi, u_lo, t_hi, t_lo, r_all, p_fwd, p_bwd,
           gradient, resist_out,
           spec, full1, full2, pair_in, part, rs_in, ping, pong, c_up, c_down, c_left, c_right, both, h_in, h, fields, power, power_in, grid, grid_in,
           row_hi, row_lo, col_hi, col_lo, ut_hi, ut_lo, r_buf, transmit,
           local_sem, pair_send, pair_recv, rs_send, rs_recv, ag_send, ag_recv):
    height, breadth = mask.shape
    tall, wide = both.shape[1:]
    kernels = h.shape[1]
    row, col = lax.axis_index("row"), lax.axis_index("kern")
    partner = 1 - col
    row_start, col_start = row * height, pl.multiple_of(col * breadth, LANES)
    slab = pl.multiple_of(breadth - LANES * col, LANES)

    local = [
        pltpu.make_async_copy(m_hi.at[pl.ds(col_start, breadth)], col_hi, local_sem.at[0]),
        pltpu.make_async_copy(m_lo.at[pl.ds(col_start, breadth)], col_lo, local_sem.at[1]),
        pltpu.make_async_copy(m_hi.at[pl.ds(row_start, height)], row_hi, local_sem.at[2]),
        pltpu.make_async_copy(m_lo.at[pl.ds(row_start, height)], row_lo, local_sem.at[3]),
        pltpu.make_async_copy(spectra, h_in, local_sem.at[4]),
        pltpu.make_async_copy(r_all.at[pl.ds(row_start + HALO, tall - HALO)], r_buf.at[pl.ds(0, tall - HALO)], local_sem.at[5]),
        pltpu.make_async_copy(r_all.at[pl.ds(row_start, HALO)], r_buf.at[pl.ds(tall - HALO, HALO)], local_sem.at[6]),
        pltpu.make_async_copy(u_hi.at[:, pl.ds(col_start, breadth)], ut_hi.at[:, pl.ds(0, breadth)], local_sem.at[7]),
        pltpu.make_async_copy(u_lo.at[:, pl.ds(col_start, breadth)], ut_lo.at[:, pl.ds(0, breadth)], local_sem.at[8]),
        pltpu.make_async_copy(u_hi.at[:, pl.ds(slab, LANES)], ut_hi.at[:, pl.ds(breadth, LANES)], local_sem.at[9]),
        pltpu.make_async_copy(u_lo.at[:, pl.ds(slab, LANES)], ut_lo.at[:, pl.ds(breadth, LANES)], local_sem.at[10]),
    ]
    for copy in local:
        copy.start()

    barrier = pltpu.get_barrier_semaphore()
    pl.semaphore_signal(barrier, inc=1, device_id={"kern": partner}, device_id_type=MESH)
    for o in range(1, rows_n):
        pl.semaphore_signal(barrier, inc=1, device_id={"row": lax.rem(row + o, rows_n)}, device_id_type=MESH)

    both[0, pl.ds(0, height), pl.ds(0, breadth)] = target[...]
    index = levels[...]
    value = jnp.zeros(index.shape, jnp.float32)
    for n in range(level_values.shape[0]):
        value = jnp.where(index == n, level_values[n], value)
    value = jnp.sqrt(value)
    block_at = lax.broadcasted_iota(jnp.int32, (index.shape[1], breadth), 0)
    pixel_at = lax.broadcasted_iota(jnp.int32, (index.shape[1], breadth), 1)
    inside = (pixel_at >= block_at * BLOCK) & (pixel_at < (block_at + 1) * BLOCK)
    inside = jnp.where(inside, 1.0, 0.0).astype(jnp.bfloat16)
    hi, lo = split(value)
    rest = (value - hi.astype(jnp.float32) - lo.astype(jnp.float32)).astype(jnp.bfloat16)
    root_rows = dot(hi, inside, NN) + dot(lo, inside, NN) + dot(rest, inside, NN)
    for b in range(index.shape[0]):
        both[1, pl.ds(b * BLOCK, BLOCK), pl.ds(0, breadth)] = jnp.broadcast_to(root_rows[b : b + 1, :], (BLOCK, breadth))
    pl.semaphore_wait(barrier, rows_n)

    def to_pair(src, dst, n):
        return pltpu.make_async_remote_copy(
            src_ref=src, dst_ref=dst, send_sem=pair_send.at[n], recv_sem=pair_recv.at[n],
            device_id={"kern": partner}, device_id_type=MESH)

    edge = pl.multiple_of((breadth - LANES) * partner, LANES)
    side = to_pair(both.at[:, pl.ds(0, height), pl.ds(edge, LANES)], both.at[:, pl.ds(0, height), pl.ds(breadth, LANES)], 0)
    side.start()

    def to_row(src, dst, peer, send, recv, n):
        return pltpu.make_async_remote_copy(
            src_ref=src, dst_ref=dst, send_sem=send.at[n], recv_sem=recv.at[n],
            device_id={"row": peer}, device_id_type=MESH)

    chunk = BAND // rows_n

    def allreduce(at, src, full, beside_pair=None, beside_scatter=None, beside_gather=None):
        swap = to_pair(src.at[pl.ds(partner * BAND, BAND)], pair_in.at[at], 1 + 2 * at)
        swap.start()
        if beside_pair is not None:
            beside_pair()
        swap.wait()
        part[at] = src[pl.ds(col * BAND, BAND)] + pair_in[at]
        copies = []
        for o in range(1, rows_n):
            peer = lax.rem(row + o, rows_n)
            copies.append(to_row(part.at[at, pl.ds(peer * chunk, chunk)], rs_in.at[at, o - 1], peer, rs_send.at[at], rs_recv.at[at], o - 1))
            copies[-1].start()
        if beside_scatter is not None:
            beside_scatter()
        for copy in copies:
            copy.wait()
        total = part[at, pl.ds(row * chunk, chunk)]
        for o in range(1, rows_n):
            total = total + rs_in[at, o - 1]
        mine = pl.ds(col * BAND + row * chunk, chunk)
        full[mine] = total
        copies = []
        for o in range(1, rows_n):
            peer = lax.rem(row + o, rows_n)
            copies.append(to_row(full.at[mine], full.at[mine], peer, ag_send.at[at], ag_recv.at[at], o - 1))
            copies[-1].start()
        if beside_gather is not None:
            beside_gather()
        for copy in copies:
            copy.wait()
        half = pl.ds(col * BAND, BAND)
        swap = to_pair(full.at[half], full.at[half], 2 + 2 * at)
        swap.start()
        swap.wait()

    scale = 1.0 / (PIXELS * BAND)
    transmit[...] = jnp.tanh(mask[...])
    for copy in local[:4]:
        copy.wait()
    col_tab = (col_hi[...], col_lo[...])
    row_tab = (row_hi[...], row_lo[...])
    halfway = dot3(split(transmit[...]), col_tab)
    prod = dot3(row_tab, split(halfway), TN)
    spec[pl.ds(0, BAND)] = (prod[:BAND, :BAND] - prod[BAND:, BAND:]) * scale
    spec[pl.ds(BAND, BAND)] = -(prod[BAND:, :BAND] + prod[:BAND, BAND:]) * scale

    def fold(first, count):
        def step(k, _):
            for c in range(2):
                hi, lo = split(h_in[c, k])
                mid = split(dot(p_fwd[...], hi, NN) + dot(p_fwd[...], lo, NN))
                h[c, k] = dot(mid[0], p_bwd[...], NN) + dot(mid[1], p_bwd[...], NN)
            return 0
        lax.fori_loop(first, first + count, step, 0)

    ends = []

    def beside_pair():
        side.wait()
        ends.append(to_row(both.at[:, pl.ds(0, HALO)], both.at[:, pl.ds(height, HALO)], lax.rem(row + rows_n - 1, rows_n), rs_send.at[2], rs_recv.at[2], 0))
        ends.append(to_row(both.at[:, pl.ds(height - HALO, HALO)], both.at[:, pl.ds(height + HALO, HALO)], lax.rem(row + 1, rows_n), rs_send.at[2], rs_recv.at[2], 1))
        for copy in ends:
            copy.start()
        for copy in local[4:]:
            copy.wait()

    allreduce(0, spec, full1, beside_pair, lambda: fold(0, kernels // 2), lambda: fold(kernels // 2, kernels - kernels // 2))

    t_tab = (t_hi[...], t_lo[...])
    r_tab = split(r_buf[...])
    power[...] = jnp.zeros_like(power)

    def forward(k, _):
        h_re, h_im = h[0, k], h[1, k]
        s_re, s_im = full1[pl.ds(0, BAND)], full1[pl.ds(BAND, BAND)]
        ee_r, eo_r, oe_r, oo_r = quads(h_re * s_re - h_im * s_im)
        ee_i, eo_i, oe_i, oo_i = quads(h_re * s_im + h_im * s_re)
        square = 0.0
        for c, m in enumerate((join(ee_r, -eo_i, -oe_i, -oo_r), join(ee_i, eo_r, oe_r, -oo_i))):
            field = dot3(split(dot3(r_tab, split(m))), t_tab)
            fields[k, c] = field
            square = square + field * field
        power[...] += weights[k] * square
        return 0

    lax.fori_loop(0, kernels, forward, 0, unroll=2)
    swap = to_pair(power, power_in, 5)
    swap.start()

    for copy in ends:
        copy.wait()
    at_row = lax.broadcasted_iota(jnp.int32, (tall, wide), 0)
    at_col = lax.broadcasted_iota(jnp.int32, (tall, wide), 1)
    first, last = row == 0, row == rows_n - 1
    outside = (at_row >= height + HALO) & first
    outside = outside | ((at_row >= height) & (at_row < height + HALO) & last)
    outside = outside | ((at_col >= breadth + LANES // 2) & (col == 0))
    outside = outside | ((at_col >= breadth) & (at_col < breadth + LANES // 2) & (col == 1))
    root = jnp.where(outside, 0.0, both[1])
    root = linear(root, height)
    rows_all = tall + 2 * HALO
    c_up[...] = root * pltpu.roll(root, 1, 0)
    c_down[...] = root * pltpu.roll(root, rows_all - 1, 0)
    c_left[...] = root * pltpu.roll(root, 1, 1)
    c_right[...] = root * pltpu.roll(root, wide - 1, 1)
    coefs = (c_up, c_down, c_left, c_right)
    pong[...] = jnp.zeros_like(pong)
    swap.wait()

    u_tab = (ut_hi[...], ut_lo[...])
    acid = dot3(split(power[...] + power_in[...]), u_tab)
    ping[...] = linear(acid, height)
    diffuse(ping, pong, coefs)
    resist = 1.0 / (1.0 + jnp.exp(-steepness * (ping[...] - threshold)))
    resist_out[...] = resist[2 * HALO : 2 * HALO + height, :breadth]
    ping[...] = 2.0 * steepness * resist * (1.0 - resist) * (resist - linear(both[0], height))
    diffuse(ping, pong, coefs)
    sens = ping[pl.ds(2 * HALO, height), pl.ds(0, breadth)]
    grid[...] = dot3(split(sens), (u_tab[0][:, :breadth], u_tab[1][:, :breadth]), NT)
    swap = to_pair(grid, grid_in, 6)
    swap.start()
    r_back = split(r_buf[pl.ds(0, height)].T)
    spec[...] = jnp.zeros_like(spec)
    swap.wait()
    grid[...] = 2.0 * (grid[...] + grid_in[...])

    def backward(k, _):
        parts = []
        for c in range(2):
            d = (weights[k] * grid[...]) * fields[k, c, pl.ds(0, height)]
            d = dot3(r_back, split(dot3(split(d), t_tab, NT)))
            parts.append((d[:HALF, :HALF], d[:HALF, HALF:], d[HALF:, :HALF], d[HALF:, HALF:]))
        (ra, rb, rc, rd), (ia, ib, ic, id_) = parts
        dg_re = spread(ra, ib, ic, -rd)
        dg_im = spread(ia, -rb, -rc, -id_)
        h_re, h_im = h[0, k], h[1, k]
        spec[pl.ds(0, BAND)] += h_re * dg_re + h_im * dg_im
        spec[pl.ds(BAND, BAND)] += h_re * dg_im - h_im * dg_re
        return 0

    lax.fori_loop(0, kernels, backward, 0, unroll=2)
    allreduce(1, spec, full2)
    ds_re, ds_im = full2[pl.ds(0, BAND)] * scale, full2[pl.ds(BAND, BAND)] * scale
    block = join(ds_re, -ds_im, -ds_im, -ds_re)
    grad = dot3(split(dot3(row_tab, split(block))), col_tab, NT)
    gradient[...] = grad * (1.0 - transmit[...] * transmit[...])


def body(mask_levels, target_image, diffusion_index, diffusion_table, kernel_weights, kernel_spectra):
    height, breadth = mask_levels.shape
    rows_n, cols_n = lax.axis_size("row"), lax.axis_size("kern")
    assert cols_n == 2
    tall, wide = height + 2 * HALO, breadth + LANES
    kernels = kernel_weights.shape[0]
    ct, st = mask_table()
    m_hi, m_lo = halves(np.concatenate([ct.T, st.T], 1))
    u_hi, u_lo = halves(interpolation_table().T)
    t_hi, t_lo = halves(half_table(np.arange(GRID) * (PIXELS // GRID)))
    r_all = jnp.asarray(half_table(np.arange(-HALO, PIXELS + HALO)).T.astype(np.float32))
    p_fwd, p_bwd = fold_matrix()
    f32, bf16 = jnp.float32, jnp.bfloat16
    vmem, hbm, smem = (pl.BlockSpec(memory_space=s) for s in (pltpu.VMEM, pl.ANY, pltpu.SMEM))
    V = pltpu.VMEM
    D = pltpu.SemaphoreType.DMA
    peers = max(rows_n - 1, 2)
    return pl.pallas_call(
        lambda *refs: kernel(rows_n, *refs),
        out_shape=(jax.ShapeDtypeStruct((height, breadth), f32),) * 2,
        in_specs=[vmem, vmem, vmem, smem, smem, hbm, hbm, hbm, hbm, hbm, vmem, vmem, hbm, vmem, vmem],
        out_specs=(vmem, vmem),
        scratch_shapes=[
            V((2 * BAND, BAND), f32), V((2 * BAND, BAND), f32), V((2 * BAND, BAND), f32),
            V((2, BAND, BAND), f32), V((2, BAND, BAND), f32), V((2, peers, BAND // rows_n, BAND), f32),
            *[V((tall + 2 * HALO, wide), f32)] * 6,
            V((2, tall, wide), f32), V(kernel_spectra.shape, f32), V(kernel_spectra.shape, f32),
            V((kernels, 2, tall, GRID), f32), V((tall, GRID), f32), V((tall, GRID), f32),
            V((height, GRID), f32), V((height, GRID), f32),
            V((height, 2 * BAND), bf16), V((height, 2 * BAND), bf16),
            V((breadth, 2 * BAND), bf16), V((breadth, 2 * BAND), bf16),
            V((GRID, wide), bf16), V((GRID, wide), bf16), V((tall, BAND), f32), V((height, breadth), f32),
            D((11,)), D((7,)), D((7,)), D((3, peers)), D((3, peers)), D((2, peers)), D((2, peers)),
        ],
        compiler_params=pltpu.CompilerParams(collective_id=0, has_side_effects=True, vmem_limit_bytes=60 * 2**20),
        name="resist_gradient",
    )(mask_levels, target_image, diffusion_index, diffusion_table, kernel_weights, kernel_spectra, m_hi, m_lo, u_hi, u_lo, t_hi, t_lo, r_all, p_fwd, p_bwd)


def solution(mesh):
    return jax.shard_map(
        body,
        mesh=mesh,
        in_specs=(
            P(("grp", "row"), "kern"),
            P(("grp", "row"), "kern"),
            P(("grp", "row"), "kern"),
            P(),
            P("kern"),
            P(None, "kern", None, None),
        ),
        out_specs=(P(("grp", "row"), "kern"), P(("grp", "row"), "kern")),
        check_vma=False,
    )
```

```python
import numpy as np
import jax
import jax.numpy as jnp
from jax import lax
from jax.experimental import pallas as pl
from jax.experimental.pallas import tpu as pltpu
from jax.sharding import PartitionSpec as P

PIXELS = 2048
BAND = 256
BLOCK = 32
STEPS = 4
HALF = BAND // 2
GRID = 2 * BAND
HALO = 2 * STEPS
LANES = 128
REAL = BAND + LANES
steepness = 8.0
threshold = 0.5
MESH = pl.DeviceIdType.MESH
NN = ((1,), (0,))
NT = ((1,), (1,))
TN = ((0,), (0,))


def mask_table():
    n = np.arange(HALF)
    pixel = np.arange(PIXELS)[:, None]
    angle = lambda f: 2 * np.pi / PIXELS * ((f[None, :] * pixel) % PIXELS)
    last = np.cos(angle(np.full(1, HALF)))
    return np.concatenate([np.cos(angle(n)), np.sin(angle(np.where(n == 0, HALF, n))), last, np.zeros((PIXELS, LANES - 1))], 1)


def unfold_matrix():
    m = np.zeros((2 * BAND, REAL))
    n = np.arange(HALF)
    m[n, n] = 1.0
    m[HALF + n[:-1], n[1:]] = 1.0
    m[BAND - 1, BAND] = 1.0
    m[BAND + n[1:], HALF + n[1:]] = 1.0
    m[BAND + HALF + n[:-1], HALF + n[1:]] = -1.0
    m[2 * BAND - 1, HALF] = -1.0
    return jnp.asarray(m.astype(jnp.bfloat16))


def half_table(positions):
    n = np.arange(HALF)
    angle = np.pi / PIXELS * (((2 * n + 1)[:, None] * positions[None, :]) % (2 * PIXELS))
    return np.concatenate([np.cos(angle), np.sin(angle)], 0)


def interpolation_table():
    d = np.arange(PIXELS)[:, None] - (PIXELS // GRID) * np.arange(GRID)[None, :]
    d = d % PIXELS
    safe = np.where(d == 0, 1, d)
    u = np.sin(2 * np.pi * ((BAND * safe) % PIXELS) / PIXELS) / (GRID * np.tan(np.pi * safe / PIXELS))
    return np.where(d == 0, 1.0, u)


def halves(x):
    x = x.astype(np.float32)
    hi = x.astype(jnp.bfloat16)
    lo = (x - hi.astype(np.float32)).astype(jnp.bfloat16)
    return jnp.asarray(hi), jnp.asarray(lo)


def fold_matrix():
    a = np.arange(BAND)
    p = np.zeros((BAND, BAND))
    p[a, np.where(a < HALF, a + HALF, BAND - 1 - a)] = 1.0
    return jnp.asarray(p.astype(jnp.bfloat16)), jnp.asarray(p.T.astype(jnp.bfloat16))


def quads(g):
    a, b, c, d = g[..., :HALF, :HALF], g[..., :HALF, HALF:], g[..., HALF:, :HALF], g[..., HALF:, HALF:]
    return a + b + c + d, a + c - b - d, a + b - c - d, a - b - c + d


def join(a, b, c, d):
    return jnp.concatenate([jnp.concatenate([a, b], -1), jnp.concatenate([c, d], -1)], -2)


def spread(ee, eo, oe, oo):
    return join(ee + eo + oe + oo, ee - eo + oe - oo, ee + eo - oe - oo, ee - eo - oe + oo)


def split(x):
    hi = x.astype(jnp.bfloat16)
    return hi, (x - hi.astype(jnp.float32)).astype(jnp.bfloat16)


def dot(a, b, dims):
    return lax.dot_general(a, b, (dims, ((), ())), preferred_element_type=jnp.float32)


def dot3(a, b, dims=NN):
    return dot(a[0], b[0], dims) + dot(a[0], b[1], dims) + dot(a[1], b[0], dims)


def diffuse(ping, pong, coefs):
    tall, wide = ping.shape[0] - 2 * HALO, ping.shape[1]

    def step(src, dst):
        for at in range(HALO, HALO + tall, 16):
            x = src[at : at + 16, :]
            here = [c[at : at + 16, :] for c in coefs]
            moved = here[0] * (src[at - 1 : at + 15, :] - x) + here[1] * (src[at + 1 : at + 17, :] - x)
            moved = moved + here[2] * (pltpu.roll(x, 1, 1) - x) + here[3] * (pltpu.roll(x, wide - 1, 1) - x)
            dst[at : at + 16, :] = x + moved

    def twice(_, carry):
        step(ping, pong)
        step(pong, ping)
        return carry

    lax.fori_loop(0, STEPS // 2, twice, 0)


def linear(x, height):
    pad = jnp.zeros((HALO, x.shape[1]), x.dtype)
    return jnp.concatenate([pad, x[height + HALO :], x[: height + HALO], pad], 0)


def pack(z, main, extra):
    main[pl.ds(0, BAND)] = z[:BAND, :LANES]
    main[pl.ds(BAND, BAND)] = z[:BAND, LANES:BAND]
    flipped = z[:, BAND:].T
    for n in range(3):
        extra[n : n + 1, :] = z[BAND : BAND + 1, n * LANES : (n + 1) * LANES]
        extra[3 + n : 4 + n, :] = flipped[0:1, n * LANES : (n + 1) * LANES]
    extra[6:8, :] = jnp.zeros((2, LANES), jnp.float32)


def unpack(main, extra):
    beside = jnp.concatenate([extra[3:4], extra[4:5]], 1)
    below = jnp.concatenate([extra[0:1], extra[1:2], extra[2:3]], 1)
    top = lambda x: jnp.where(lax.broadcasted_iota(jnp.int32, (LANES, x.shape[1]), 0) == 0, jnp.broadcast_to(x, (LANES, x.shape[1])), 0.0)
    upper = jnp.concatenate([main[pl.ds(0, BAND)], main[pl.ds(BAND, BAND)], top(beside).T], 1)
    return jnp.concatenate([upper, top(below)], 0)


def kernel(rows_n, mask, target, levels, level_values, weights, spectra, m_hi, m_lo, u_hi, u_lo, t_hi, t_lo, r_all, p_fwd, p_bwd, unfold,
           gradient, resist_out,
           spec, main, full1, full2, ext, ext_in, ext_part, ext_rows, pair_in, part, rs_in, ping, pong, c_up, c_down, c_left, c_right, both, h_in, h, fields, power, power_in, grid, grid_in,
           row_hi, row_lo, col_hi, col_lo, ut_hi, ut_lo, r_buf, transmit,
           local_sem, pair_send, pair_recv, rs_send, rs_recv, ag_send, ag_recv, ext_send, ext_recv):
    height, breadth = mask.shape
    tall, wide = both.shape[1:]
    kernels = h.shape[1]
    row, col = lax.axis_index("row"), lax.axis_index("kern")
    partner = 1 - col
    row_start, col_start = row * height, pl.multiple_of(col * breadth, LANES)
    slab = pl.multiple_of(breadth - LANES * col, LANES)

    local = [
        pltpu.make_async_copy(m_hi.at[pl.ds(col_start, breadth)], col_hi, local_sem.at[0]),
        pltpu.make_async_copy(m_lo.at[pl.ds(col_start, breadth)], col_lo, local_sem.at[1]),
        pltpu.make_async_copy(m_hi.at[pl.ds(row_start, height)], row_hi, local_sem.at[2]),
        pltpu.make_async_copy(m_lo.at[pl.ds(row_start, height)], row_lo, local_sem.at[3]),
        pltpu.make_async_copy(spectra, h_in, local_sem.at[4]),
        pltpu.make_async_copy(r_all.at[pl.ds(row_start + HALO, tall - HALO)], r_buf.at[pl.ds(0, tall - HALO)], local_sem.at[5]),
        pltpu.make_async_copy(r_all.at[pl.ds(row_start, HALO)], r_buf.at[pl.ds(tall - HALO, HALO)], local_sem.at[6]),
        pltpu.make_async_copy(u_hi.at[:, pl.ds(col_start, breadth)], ut_hi.at[:, pl.ds(0, breadth)], local_sem.at[7]),
        pltpu.make_async_copy(u_lo.at[:, pl.ds(col_start, breadth)], ut_lo.at[:, pl.ds(0, breadth)], local_sem.at[8]),
        pltpu.make_async_copy(u_hi.at[:, pl.ds(slab, LANES)], ut_hi.at[:, pl.ds(breadth, LANES)], local_sem.at[9]),
        pltpu.make_async_copy(u_lo.at[:, pl.ds(slab, LANES)], ut_lo.at[:, pl.ds(breadth, LANES)], local_sem.at[10]),
    ]
    for copy in local:
        copy.start()

    barrier = pltpu.get_barrier_semaphore()
    pl.semaphore_signal(barrier, inc=1, device_id={"kern": partner}, device_id_type=MESH)
    for o in range(1, rows_n):
        pl.semaphore_signal(barrier, inc=1, device_id={"row": lax.rem(row + o, rows_n)}, device_id_type=MESH)

    both[0, pl.ds(0, height), pl.ds(0, breadth)] = target[...]
    index = levels[...]
    value = jnp.zeros(index.shape, jnp.float32)
    for n in range(level_values.shape[0]):
        value = jnp.where(index == n, level_values[n], value)
    value = jnp.sqrt(value)
    block_at = lax.broadcasted_iota(jnp.int32, (index.shape[1], breadth), 0)
    pixel_at = lax.broadcasted_iota(jnp.int32, (index.shape[1], breadth), 1)
    inside = (pixel_at >= block_at * BLOCK) & (pixel_at < (block_at + 1) * BLOCK)
    inside = jnp.where(inside, 1.0, 0.0).astype(jnp.bfloat16)
    hi, lo = split(value)
    rest = (value - hi.astype(jnp.float32) - lo.astype(jnp.float32)).astype(jnp.bfloat16)
    root_rows = dot(hi, inside, NN) + dot(lo, inside, NN) + dot(rest, inside, NN)
    for b in range(index.shape[0]):
        both[1, pl.ds(b * BLOCK, BLOCK), pl.ds(0, breadth)] = jnp.broadcast_to(root_rows[b : b + 1, :], (BLOCK, breadth))
    pl.semaphore_wait(barrier, rows_n)

    def to_pair(src, dst, n):
        return pltpu.make_async_remote_copy(
            src_ref=src, dst_ref=dst, send_sem=pair_send.at[n], recv_sem=pair_recv.at[n],
            device_id={"kern": partner}, device_id_type=MESH)

    edge = pl.multiple_of((breadth - LANES) * partner, LANES)
    side = to_pair(both.at[:, pl.ds(0, height), pl.ds(edge, LANES)], both.at[:, pl.ds(0, height), pl.ds(breadth, LANES)], 0)
    side.start()

    def to_row(src, dst, peer, send, recv, n):
        return pltpu.make_async_remote_copy(
            src_ref=src, dst_ref=dst, send_sem=send.at[n], recv_sem=recv.at[n],
            device_id={"row": peer}, device_id_type=MESH)

    chunk = BAND // rows_n

    def allreduce(at, src, full, beside_pair=None, beside_scatter=None, beside_gather=None):
        swap = to_pair(src.at[pl.ds(partner * BAND, BAND)], pair_in.at[at], 1 + 2 * at)
        swap.start()
        ext_swap = to_pair(ext.at[at], ext_in.at[at], 7 + at)
        ext_swap.start()
        if beside_pair is not None:
            beside_pair()
        swap.wait()
        ext_swap.wait()
        ext_part[at] = ext[at] + ext_in[at]
        part[at] = src[pl.ds(col * BAND, BAND)] + pair_in[at]
        copies = []
        for o in range(1, rows_n):
            peer = lax.rem(row + o, rows_n)
            copies.append(to_row(part.at[at, pl.ds(peer * chunk, chunk)], rs_in.at[at, o - 1], peer, rs_send.at[at], rs_recv.at[at], o - 1))
            copies[-1].start()
        for o in range(1, rows_n):
            peer = lax.rem(row + o, rows_n)
            copies.append(to_row(ext_part.at[at], ext_rows.at[at, o - 1], peer, ext_send.at[at], ext_recv.at[at], o - 1))
            copies[-1].start()
        if beside_scatter is not None:
            beside_scatter()
        for copy in copies:
            copy.wait()
        total = part[at, pl.ds(row * chunk, chunk)]
        for o in range(1, rows_n):
            total = total + rs_in[at, o - 1]
        mine = pl.ds(col * BAND + row * chunk, chunk)
        full[mine] = total
        copies = []
        for o in range(1, rows_n):
            peer = lax.rem(row + o, rows_n)
            copies.append(to_row(full.at[mine], full.at[mine], peer, ag_send.at[at], ag_recv.at[at], o - 1))
            copies[-1].start()
        if beside_gather is not None:
            beside_gather()
        for copy in copies:
            copy.wait()
        half = pl.ds(col * BAND, BAND)
        swap = to_pair(full.at[half], full.at[half], 2 + 2 * at)
        swap.start()
        extra = ext_part[at]
        for o in range(1, rows_n):
            extra = extra + ext_rows[at, o - 1]
        swap.wait()
        return unpack(full, extra)

    scale = 1.0 / (PIXELS * BAND)
    transmit[...] = jnp.tanh(mask[...])
    for copy in local[:4]:
        copy.wait()
    col_tab = (col_hi[...], col_lo[...])
    row_tab = (row_hi[...], row_lo[...])
    halfway = dot3(split(transmit[...]), col_tab)
    prod = dot3(row_tab, split(halfway), TN)
    pack(prod, main, ext.at[0])

    def fold(first, count):
        def step(k, _):
            for c in range(2):
                hi, lo = split(h_in[c, k])
                mid = split(dot(p_fwd[...], hi, NN) + dot(p_fwd[...], lo, NN))
                h[c, k] = dot(mid[0], p_bwd[...], NN) + dot(mid[1], p_bwd[...], NN)
            return 0
        lax.fori_loop(first, first + count, step, 0)

    ends = []

    def beside_pair():
        side.wait()
        ends.append(to_row(both.at[:, pl.ds(0, HALO)], both.at[:, pl.ds(height, HALO)], lax.rem(row + rows_n - 1, rows_n), rs_send.at[2], rs_recv.at[2], 0))
        ends.append(to_row(both.at[:, pl.ds(height - HALO, HALO)], both.at[:, pl.ds(height + HALO, HALO)], lax.rem(row + 1, rows_n), rs_send.at[2], rs_recv.at[2], 1))
        for copy in ends:
            copy.start()
        for copy in local[4:]:
            copy.wait()

    real = allreduce(0, main, full1, beside_pair, lambda: fold(0, kernels // 2), lambda: fold(kernels // 2, kernels - kernels // 2))

    real = split(real)
    half_way = split(dot(unfold[...], real[0], NN) + dot(unfold[...], real[1], NN))
    prod = dot(half_way[0], unfold[...], NT) + dot(half_way[1], unfold[...], NT)
    spec[pl.ds(0, BAND)] = (prod[:BAND, :BAND] - prod[BAND:, BAND:]) * scale
    spec[pl.ds(BAND, BAND)] = -(prod[BAND:, :BAND] + prod[:BAND, BAND:]) * scale

    t_tab = (t_hi[...], t_lo[...])
    r_tab = split(r_buf[...])
    power[...] = jnp.zeros_like(power)

    def forward(k, _):
        h_re, h_im = h[0, k], h[1, k]
        s_re, s_im = spec[pl.ds(0, BAND)], spec[pl.ds(BAND, BAND)]
        ee_r, eo_r, oe_r, oo_r = quads(h_re * s_re - h_im * s_im)
        ee_i, eo_i, oe_i, oo_i = quads(h_re * s_im + h_im * s_re)
        square = 0.0
        for c, m in enumerate((join(ee_r, -eo_i, -oe_i, -oo_r), join(ee_i, eo_r, oe_r, -oo_i))):
            field = dot3(split(dot3(r_tab, split(m))), t_tab)
            fields[k, c] = field
            square = square + field * field
        power[...] += weights[k] * square
        return 0

    lax.fori_loop(0, kernels, forward, 0, unroll=2)
    swap = to_pair(power, power_in, 5)
    swap.start()

    for copy in ends:
        copy.wait()
    at_row = lax.broadcasted_iota(jnp.int32, (tall, wide), 0)
    at_col = lax.broadcasted_iota(jnp.int32, (tall, wide), 1)
    first, last = row == 0, row == rows_n - 1
    outside = (at_row >= height + HALO) & first
    outside = outside | ((at_row >= height) & (at_row < height + HALO) & last)
    outside = outside | ((at_col >= breadth + LANES // 2) & (col == 0))
    outside = outside | ((at_col >= breadth) & (at_col < breadth + LANES // 2) & (col == 1))
    root = jnp.where(outside, 0.0, both[1])
    root = linear(root, height)
    rows_all = tall + 2 * HALO
    c_up[...] = root * pltpu.roll(root, 1, 0)
    c_down[...] = root * pltpu.roll(root, rows_all - 1, 0)
    c_left[...] = root * pltpu.roll(root, 1, 1)
    c_right[...] = root * pltpu.roll(root, wide - 1, 1)
    coefs = (c_up, c_down, c_left, c_right)
    pong[...] = jnp.zeros_like(pong)
    swap.wait()

    u_tab = (ut_hi[...], ut_lo[...])
    acid = dot3(split(power[...] + power_in[...]), u_tab)
    ping[...] = linear(acid, height)
    diffuse(ping, pong, coefs)
    resist = 1.0 / (1.0 + jnp.exp(-steepness * (ping[...] - threshold)))
    resist_out[...] = resist[2 * HALO : 2 * HALO + height, :breadth]
    ping[...] = 2.0 * steepness * resist * (1.0 - resist) * (resist - linear(both[0], height))
    diffuse(ping, pong, coefs)
    sens = ping[pl.ds(2 * HALO, height), pl.ds(0, breadth)]
    grid[...] = dot3(split(sens), (u_tab[0][:, :breadth], u_tab[1][:, :breadth]), NT)
    swap = to_pair(grid, grid_in, 6)
    swap.start()
    r_back = split(r_buf[pl.ds(0, height)].T)
    spec[...] = jnp.zeros_like(spec)
    swap.wait()
    grid[...] = 2.0 * (grid[...] + grid_in[...])

    def backward(k, _):
        parts = []
        for c in range(2):
            d = (weights[k] * grid[...]) * fields[k, c, pl.ds(0, height)]
            d = dot3(r_back, split(dot3(split(d), t_tab, NT)))
            parts.append((d[:HALF, :HALF], d[:HALF, HALF:], d[HALF:, :HALF], d[HALF:, HALF:]))
        (ra, rb, rc, rd), (ia, ib, ic, id_) = parts
        dg_re = spread(ra, ib, ic, -rd)
        dg_im = spread(ia, -rb, -rc, -id_)
        h_re, h_im = h[0, k], h[1, k]
        spec[pl.ds(0, BAND)] += h_re * dg_re + h_im * dg_im
        spec[pl.ds(BAND, BAND)] += h_re * dg_im - h_im * dg_re
        return 0

    lax.fori_loop(0, kernels, backward, 0, unroll=2)
    ds_re, ds_im = spec[pl.ds(0, BAND)] * scale, spec[pl.ds(BAND, BAND)] * scale
    block = split(join(ds_re, -ds_im, -ds_im, -ds_re))
    half_way = split(dot(block[0], unfold[...], NN) + dot(block[1], unfold[...], NN))
    pack(dot(unfold[...], half_way[0], TN) + dot(unfold[...], half_way[1], TN), main, ext.at[1])
    real = allreduce(1, main, full2)
    grad = dot3(split(dot3(row_tab, split(real))), col_tab, NT)
    gradient[...] = grad * (1.0 - transmit[...] * transmit[...])


def body(mask_levels, target_image, diffusion_index, diffusion_table, kernel_weights, kernel_spectra):
    height, breadth = mask_levels.shape
    rows_n, cols_n = lax.axis_size("row"), lax.axis_size("kern")
    assert cols_n == 2
    tall, wide = height + 2 * HALO, breadth + LANES
    kernels = kernel_weights.shape[0]
    m_hi, m_lo = halves(mask_table())
    u_hi, u_lo = halves(interpolation_table().T)
    t_hi, t_lo = halves(half_table(np.arange(GRID) * (PIXELS // GRID)))
    r_all = jnp.asarray(half_table(np.arange(-HALO, PIXELS + HALO)).T.astype(np.float32))
    p_fwd, p_bwd = fold_matrix()
    f32, bf16 = jnp.float32, jnp.bfloat16
    vmem, hbm, smem = (pl.BlockSpec(memory_space=s) for s in (pltpu.VMEM, pl.ANY, pltpu.SMEM))
    V = pltpu.VMEM
    D = pltpu.SemaphoreType.DMA
    peers = max(rows_n - 1, 2)
    return pl.pallas_call(
        lambda *refs: kernel(rows_n, *refs),
        out_shape=(jax.ShapeDtypeStruct((height, breadth), f32),) * 2,
        in_specs=[vmem, vmem, vmem, smem, smem, hbm, hbm, hbm, hbm, hbm, vmem, vmem, hbm, vmem, vmem, vmem],
        out_specs=(vmem, vmem),
        scratch_shapes=[
            V((2 * BAND, BAND), f32), *[V((2 * BAND, LANES), f32)] * 3,
            *[V((2, 8, LANES), f32)] * 3, V((2, peers, 8, LANES), f32),
            V((2, BAND, LANES), f32), V((2, BAND, LANES), f32), V((2, peers, BAND // rows_n, LANES), f32),
            *[V((tall + 2 * HALO, wide), f32)] * 6,
            V((2, tall, wide), f32), V(kernel_spectra.shape, f32), V(kernel_spectra.shape, f32),
            V((kernels, 2, tall, GRID), f32), V((tall, GRID), f32), V((tall, GRID), f32),
            V((height, GRID), f32), V((height, GRID), f32),
            V((height, REAL), bf16), V((height, REAL), bf16),
            V((breadth, REAL), bf16), V((breadth, REAL), bf16),
            V((GRID, wide), bf16), V((GRID, wide), bf16), V((tall, BAND), f32), V((height, breadth), f32),
            D((11,)), D((9,)), D((9,)), D((3, peers)), D((3, peers)), *[D((2, peers))] * 4,
        ],
        compiler_params=pltpu.CompilerParams(collective_id=0, has_side_effects=True, vmem_limit_bytes=60 * 2**20),
        name="resist_gradient",
    )(mask_levels, target_image, diffusion_index, diffusion_table, kernel_weights, kernel_spectra, m_hi, m_lo, u_hi, u_lo, t_hi, t_lo, r_all, p_fwd, p_bwd, unfold_matrix())


def solution(mesh):
    return jax.shard_map(
        body,
        mesh=mesh,
        in_specs=(
            P(("grp", "row"), "kern"),
            P(("grp", "row"), "kern"),
            P(("grp", "row"), "kern"),
            P(),
            P("kern"),
            P(None, "kern", None, None),
        ),
        out_specs=(P(("grp", "row"), "kern"), P(("grp", "row"), "kern")),
        check_vma=False,
    )
```
